32 devices in a mesh: groups: 2 (over x), lon: 16 (over z, y, core).
Axes of the slice: x: 2, y: 2, z: 4, core: 2. Of those that a mesh axis runs over, the one named last changes fastest.
Arguments:
- observations: bfloat16 [32768, 128], P(('groups', 'lon')), parts along dimension 0, may hold values from -6 to 6
- cell_index: int32 [32768], P(('groups', 'lon')), parts along dimension 0, may hold values from 0 to 1023
- tile_counts: int32 [32, 16], P(('groups', 'lon')), parts along dimension 0, may hold values from 0 to 128, as said below
- enc_weight: bfloat16 [128, 384], replicated, may hold values from -0.5 to 0.5
- conv_weight: bfloat16 [3, 3, 384, 384], replicated, may hold values from -0.109375 to 0.109375
- cotangent: bfloat16 [128, 256, 384], P('groups', 'lon'), parts along dimension 0, may hold values from -6 to 6
Outputs:
- features: bfloat16 [128, 256, 384], P('groups', 'lon'), parts along dimension 0
- obs_grad: bfloat16 [32768, 128], P(('groups', 'lon')), parts along dimension 0
- conv_grad: bfloat16 [6, 3, 384, 384], P('groups'), parts along dimension 0
- enc_grad: bfloat16 [256, 384], P('groups'), parts along dimension 0
The draws below stay inside these ranges and needn't reach their ends.
There are 2 independent parts, one for each index of `groups`. The reference program is written for one: setup_inputs(seed, part) draws one part's arguments, and reference() takes and returns one part's arrays. A program takes and returns all parts, laid end to end along the dimension named above; an argument that names none is the same for every part. Nothing has to cross between parts.
Inputs may be any that keep to these rules, and one draw needn't show every extreme that they name: `tile_counts`: each row sums to 1024; the observations of device s come in runs by destination tile in ascending order with these lengths; in every draw one tile receives exactly 128 observations from every device.
All inputs are finite; a program needn't handle non-finite values.
Results may differ from the reference program's by a relative error of at most 0.0054.
Values may be sent and summed in bfloat16 or wider, within the bound.
A program may use at most 128 MiB of HBM per device.

```python
import jax
import jax.numpy as jnp

C = 384
K = 128
LAT = 64
LON_DEV = 16
OBS_DEV = 1024
CAP = 128
LON = 256
OBS = 16384
N_LON = 16


def draw_tile_counts(key, part):
    key = jax.random.fold_in(key, 11)
    half = CAP // 2
    hot = jax.random.randint(jax.random.fold_in(key, 1), (), 0, N_LON)
    row_keys = jax.random.split(jax.random.fold_in(key, 2), N_LON)

    def one_row(row_key):
        key_a, key_b = jax.random.split(row_key)
        order = jax.random.permutation(key_a, N_LON)
        moved = jax.random.randint(key_b, (N_LON // 2,), 1 - half, half + 1)
        delta = jnp.zeros((N_LON,), jnp.int32).at[order[0::2]].set(moved).at[order[1::2]].set(-moved)
        place = jnp.argmax((order == hot).astype(jnp.int32))
        partner = order[jnp.bitwise_xor(place, 1)]
        delta = delta.at[hot].set(half).at[partner].set(-half)
        return half + delta
    return jax.vmap(one_row)(row_keys).astype(jnp.int32)


def plant(result, own_key, least, high):
    longest = result.shape.index(max(result.shape))
    spots = []
    for shift in (0, 1):
        where = [jax.random.randint(jax.random.fold_in(own_key, axis), (), 0, length) for axis, length in enumerate(result.shape)]
        where[longest] = (where[longest] + shift) % result.shape[longest]
        spots.append(tuple(where))
    return result.at[spots[0]].set(least).at[spots[1]].set(high)


def shard_levels(key, shape, pieces, smallest, high):
    def one(position, parts):
        steps = jax.random.uniform(jax.random.fold_in(jax.random.fold_in(key, 6), position), (parts,), jnp.float32, smallest / len(pieces), high / len(pieces))
        return jnp.repeat(jnp.exp(steps), shape[position] // parts).reshape((-1,) + (1,) * (len(shape) - position - 1))

    factor_of = one(*pieces[0])
    for cut in pieces[1:]:
        factor_of = factor_of * one(*cut)
    return factor_of


def noise(key, dims, deviation, limit, cuts=(), kind=jnp.bfloat16):
    entries = deviation * jax.random.normal(key, dims, jnp.float32)
    if cuts:
        entries = entries * shard_levels(key, dims, cuts, -0.22, 0.18)
    return jnp.clip(entries, -limit, limit).astype(kind)


def setup_inputs(seed: int = 0, part: int = 0) -> dict:
    seeds = jax.random.split(jax.random.key(seed), 7)
    part_keys = jax.random.split(jax.random.fold_in(seeds[6], part), 7)
    observations = noise(part_keys[0], (OBS, K), 1.0, 6.0, ((0, 16),))
    cell_index = plant(jax.random.randint(part_keys[1], (OBS,), 0, LAT * LON_DEV), jax.random.fold_in(part_keys[1], 1), 0, (LAT * LON_DEV) - 1).astype(jnp.int32)
    tile_counts = draw_tile_counts(jax.random.fold_in(jax.random.fold_in(seeds[6], part), 71), part)
    enc_weight = noise(seeds[3], (K, C), K ** -0.5, 0.5)
    conv_weight = noise(seeds[4], (3, 3, C, C), (9 * C) ** -0.5, 0.109375)
    cotangent = noise(part_keys[5], (LAT, LON, C), 1.0, 6.0, ((1, 16),))
    return dict(observations=observations, cell_index=cell_index, tile_counts=tile_counts, enc_weight=enc_weight, conv_weight=conv_weight, cotangent=cotangent)


def pad_grid(grid):
    wrapped = jnp.concatenate([grid[:, -1:], grid, grid[:, :1]], axis=1)
    return jnp.pad(wrapped, ((1, 1), (0, 0), (0, 0)))

def logistic_grad(pre):
    sig = jax.nn.sigmoid(pre)
    return sig * (1.0 + pre * (1.0 - sig))

def reference(observations, cell_index, tile_counts, enc_weight, conv_weight, cotangent):
    tiles = jnp.arange(N_LON, dtype=jnp.int32)
    dest = jax.vmap(lambda row: jnp.repeat(tiles, row, total_repeat_length=OBS_DEV))(tile_counts).reshape(-1).astype(jnp.int32)
    lat_row = cell_index // LON_DEV
    lon_col = dest * LON_DEV + cell_index % LON_DEV
    flat = (lat_row * LON + lon_col).astype(jnp.int32)
    ncell = LAT * LON
    raw_sum = jax.ops.segment_sum(observations.astype(jnp.float32), flat, ncell)
    count = jax.ops.segment_sum(jnp.ones_like(flat), flat, ncell)
    denom = jnp.maximum(count, 1).astype(jnp.float32)[:, None]
    raw_mean = (raw_sum / denom).astype(jnp.bfloat16)
    pre = jnp.dot(raw_mean, enc_weight, preferred_element_type=jnp.float32)
    encoded = jax.nn.silu(pre).astype(jnp.bfloat16).reshape(LAT, LON, C)
    xpad = pad_grid(encoded)
    gpad = pad_grid(cotangent)
    cot_flat = cotangent.reshape(-1, C)
    out = jnp.zeros((ncell, C), jnp.float32)
    d_enc = jnp.zeros((ncell, C), jnp.float32)
    taps = []
    for a in range(3):
        row_taps = []
        for b in range(3):
            window = xpad[a:a + LAT, b:b + LON].reshape(-1, C)
            out = out + jnp.dot(window, conv_weight[a, b], preferred_element_type=jnp.float32)
            back = gpad[2 - a:2 - a + LAT, 2 - b:2 - b + LON].reshape(-1, C)
            d_enc = d_enc + jnp.dot(back, conv_weight[a, b].T, preferred_element_type=jnp.float32)
            row_taps.append(jnp.dot(window.T, cot_flat, preferred_element_type=jnp.float32))
        taps.append(jnp.stack(row_taps))
    conv_raw = jnp.stack(taps)
    features = out.astype(jnp.bfloat16).reshape(LAT, LON, C)
    d_pre = (d_enc * logistic_grad(pre)).astype(jnp.bfloat16)
    enc_raw = jnp.dot(raw_mean.T, d_pre, preferred_element_type=jnp.float32)
    d_raw = jnp.dot(d_pre, enc_weight.T, preferred_element_type=jnp.float32)
    cell_grad = (d_raw / denom).astype(jnp.bfloat16)
    obs_grad = cell_grad[flat]
    norm = jnp.sqrt(jnp.sum(conv_raw * conv_raw) + jnp.sum(enc_raw * enc_raw))
    scale = jnp.minimum(1.0, 1.0 / (norm + 1e-06))
    return (features, obs_grad, (conv_raw * scale).astype(jnp.bfloat16), (enc_raw * scale).astype(jnp.bfloat16))
```

```python
import functools

import jax
import jax.numpy as jnp
from jax import lax
from jax.experimental import pallas as pl
from jax.experimental.pallas import tpu as pltpu
from jax.sharding import PartitionSpec as P

F32, BF16 = jnp.float32, jnp.bfloat16
VMEM = pl.BlockSpec(memory_space=pltpu.VMEM)
LIMIT = 48 * 2**20


def dot(a, b):
    return jnp.dot(a, b, preferred_element_type=F32)


def dot_t(a, b):
    return lax.dot_general(a, b, (((1,), (1,)), ((), ())), preferred_element_type=F32)


def encode_kernel(cells_ref, rows_ref, weight_ref, mean_ref, denom_ref, pre_ref, enc_ref, total):
    blocks, width = cells_ref.shape
    ncell, feats = mean_ref.shape
    total[...] = jnp.zeros_like(total)
    ones = jnp.ones((width, feats), BF16)

    def body(i, _):
        ids = lax.broadcasted_iota(jnp.int32, (ncell, width), 0)
        match = (ids == cells_ref[pl.ds(i, 1), :]).astype(F32).astype(BF16)
        rows = rows_ref[pl.ds(pl.multiple_of(i * width, width), width), :]
        total[...] += dot(match, jnp.concatenate([rows, ones], axis=1))
        return 0

    lax.fori_loop(0, blocks, body, 0)
    denom = jnp.maximum(total[:, feats:], 1.0)
    mean = (total[:, :feats] / denom).astype(BF16)
    mean_ref[...] = mean
    denom_ref[...] = denom
    pre = dot(mean, weight_ref[...])
    pre_ref[...] = pre
    enc_ref[...] = (pre * jax.nn.sigmoid(pre)).astype(BF16)


def pick_kernel(cells_ref, grad_ref, out_ref, grad_t):
    blocks, width = cells_ref.shape
    ncell, feats = grad_ref.shape
    grad_t[...] = grad_ref[...].T

    def body(i, _):
        ids = lax.broadcasted_iota(jnp.int32, (ncell, width), 0)
        match = (ids == cells_ref[pl.ds(i, 1), :]).astype(F32).astype(BF16)
        out = dot(grad_t[...], match)
        out_ref[pl.ds(pl.multiple_of(i * width, width), width), :] = out.T.astype(BF16)
        return 0

    lax.fori_loop(0, blocks, body, 0)


def plan(n, need):
    unit = 16 * n
    units = -(-need // unit)
    streams = min(4, units)
    sizes = [unit * (units // streams + (1 if i < units % streams else 0)) for i in range(streams)]
    return sizes


def conv_kernel(
    n, sizes, xb, gb, w, pre_ref, mean_ref, denom_ref, ew_ref,
    feat_ref, cell_ref, sum_ref,
    xt, acc, denc, sbuf, rbuf, rs_send, rs_recv, ag_send, ag_recv,
):
    lane = xb.shape[2]
    lat16 = pre_ref.shape[0]
    cols = (xb.shape[1] - lat16) // 2
    feats = mean_ref.shape[1]
    taps = 9
    me = lax.axis_index("lon")
    levels = n.bit_length() - 1

    def bit_of(k):
        return lax.rem(me // (2**k), 2)

    def partner(k):
        return me + (1 - 2 * bit_of(k)) * (2**k)

    barrier = pltpu.get_barrier_semaphore()
    for k in range(levels):
        pl.semaphore_signal(
            barrier, inc=1, device_id={"lon": partner(k)}, device_id_type=pl.DeviceIdType.MESH
        )
    pl.semaphore_wait(barrier, levels)

    starts, ranges = [], []
    base = 0
    for s, size in enumerate(sizes):
        order = list(range(levels))
        if s % 2 and levels > 2:
            order = [0] + order[2:] + [1]
        off, length, stages = base, size, []
        for k in order:
            half = length // 2
            b = bit_of(k)
            keep = pl.multiple_of(off + b * half, 16)
            send = pl.multiple_of(off + (1 - b) * half, 16)
            stages.append((k, keep, send, half))
            off, length = keep, half
        starts.append(base)
        ranges.append(stages)
        base += size
    ends = [a + b for a, b in zip(starts, sizes)]

    copies = []
    pos = [0] * len(sizes)
    flying = [None] * len(sizes)

    def send_sum(s, j):
        k, keep, send, half = ranges[s][j]
        sbuf[pl.ds(send, half), :] = acc[pl.ds(send, half), :].astype(BF16)
        copy = pltpu.make_async_remote_copy(
            src_ref=sbuf.at[pl.ds(send, half), :],
            dst_ref=rbuf.at[pl.ds(keep, half), :],
            send_sem=rs_send.at[s, j], recv_sem=rs_recv.at[s, j],
            device_id={"lon": partner(k)}, device_id_type=pl.DeviceIdType.MESH,
        )
        copy.start()
        copies.append(copy)
        flying[s] = copy

    def send_result(s, j):
        k, keep, send, half = ranges[s][j]
        copy = pltpu.make_async_remote_copy(
            src_ref=sum_ref.at[pl.ds(keep, half), :],
            dst_ref=sum_ref.at[pl.ds(keep, half), :],
            send_sem=ag_send.at[s, j], recv_sem=ag_recv.at[s, j],
            device_id={"lon": partner(k)}, device_id_type=pl.DeviceIdType.MESH,
        )
        copy.start()
        copies.append(copy)
        flying[s] = copy

    def begin(s):
        send_sum(s, 0)

    def step(s):
        p = pos[s]
        if p >= 2 * levels:
            return
        flying[s].wait_recv()
        if p < levels:
            k, keep, send, half = ranges[s][p]
            value = acc[pl.ds(keep, half), :] + rbuf[pl.ds(send, half), :].astype(F32)
            if p + 1 < levels:
                acc[pl.ds(keep, half), :] = value
                send_sum(s, p + 1)
            else:
                sum_ref[pl.ds(keep, half), :] = value.astype(BF16)
                send_result(s, levels - 1)
        else:
            j = 2 * levels - 1 - p
            if j > 0:
                send_result(s, j - 1)
        pos[s] = p + 1

    for b in range(3):
        xt[b] = xb[b, pl.ds(cols, lat16), :].T

    def raw_tap(t, _):
        a, b = t // 3, lax.rem(t, 3)
        grad = gb[1, pl.ds(pl.multiple_of((2 - a) * cols, 16), lat16), :]
        acc[pl.ds(pl.multiple_of(t * lane, 16), lane), :] = dot(xt[b], grad)
        return 0

    tile = min(256, lat16)
    tiles = lat16 // tile

    def denc_tile(r, _):
        total = None
        for t in range(taps):
            a, b = t // 3, t % 3
            rows = gb[2 - b, pl.ds(pl.multiple_of((2 - a) * cols + r * tile, 16), tile), :]
            part = dot_t(rows, w[t * lane : (t + 1) * lane, :])
            total = part if total is None else total + part
        here = pl.ds(pl.multiple_of(r * tile, 16), tile)
        pre = pre_ref[here, :]
        sig = jax.nn.sigmoid(pre)
        d_pre = (total * (sig * (1.0 + pre * (1.0 - sig)))).astype(BF16)
        denc[here, :] = d_pre
        cell_ref[here, :] = (dot_t(d_pre, ew_ref[...]) / denom_ref[here, :]).astype(BF16)
        return 0

    def feat_tile(r, _):
        total = None
        for t in range(taps):
            a, b = t // 3, t % 3
            rows = xb[b, pl.ds(pl.multiple_of(a * cols + r * tile, 16), tile), :]
            part = dot(rows, w[t * lane : (t + 1) * lane, :])
            total = part if total is None else total + part
        feat_ref[pl.ds(pl.multiple_of(r * tile, 16), tile), :] = total.astype(BF16)
        return 0

    last = len(sizes) - 1
    done = 0
    for s in range(last):
        upto = min(taps, -(-ends[s] // lane))
        lax.fori_loop(done, upto, raw_tap, 0)
        done = upto
        begin(s)
    if done < taps:
        lax.fori_loop(done, taps, raw_tap, 0)
    for r in range(0, tiles, 2):
        lax.fori_loop(r, min(r + 2, tiles), denc_tile, 0)
        for s in range(last):
            step(s)
    acc[taps * lane : taps * lane + feats, :] = lax.dot_general(
        mean_ref[...], denc[...], (((0,), (0,)), ((), ())), preferred_element_type=F32
    )
    if taps * lane + feats < base:
        acc[taps * lane + feats : base, :] = jnp.zeros((base - taps * lane - feats, lane), F32)
    begin(last)
    for r in range(0, tiles, 2):
        lax.fori_loop(r, min(r + 2, tiles), feat_tile, 0)
        for s in range(last + 1):
            step(s)
    while min(pos) < 2 * levels:
        for s in range(last + 1):
            step(s)
    for copy in copies:
        copy.wait_send()


def conv_call(n, xb, gb, w, pre, mean, denom, ew):
    lane = xb.shape[2]
    ncell, feats = mean.shape
    need = 9 * lane + feats
    sizes = plan(n, need)
    rows = sum(sizes)
    levels = n.bit_length() - 1
    sems = pltpu.SemaphoreType.DMA((len(sizes), levels))
    return pl.pallas_call(
        functools.partial(conv_kernel, n, sizes),
        out_shape=(
            jax.ShapeDtypeStruct((ncell, lane), BF16),
            jax.ShapeDtypeStruct((ncell, feats), BF16),
            jax.ShapeDtypeStruct((rows, lane), BF16),
        ),
        in_specs=[VMEM] * 7,
        out_specs=(VMEM,) * 3,
        scratch_shapes=[
            pltpu.VMEM((3, lane, ncell), BF16),
            pltpu.VMEM((rows, lane), F32),
            pltpu.VMEM((ncell, lane), BF16),
            pltpu.VMEM((rows, lane), BF16),
            pltpu.VMEM((rows, lane), BF16),
            sems, sems, sems, sems,
        ],
        compiler_params=pltpu.CompilerParams(
            collective_id=0, has_side_effects=True, vmem_limit_bytes=LIMIT
        ),
        name="conv",
    )(xb, gb, w, pre, mean, denom, ew)


def shifted(grid, ntiles):
    up = [(i, (i + 1) % ntiles) for i in range(ntiles)]
    down = [(j, i) for i, j in up]
    before = lax.ppermute(grid[:, -1:], "lon", up)
    after = lax.ppermute(grid[:, :1], "lon", down)
    views = jnp.stack([
        jnp.concatenate([before, grid[:, :-1]], axis=1),
        grid,
        jnp.concatenate([grid[:, 1:], after], axis=1),
    ])
    views = jnp.pad(views, ((0, 0), (1, 1), (0, 0), (0, 0)))
    return views.reshape(3, -1, grid.shape[-1])


def per_device(observations, cell_index, tile_counts, enc_weight, conv_weight, cotangent):
    lat_rows, lon_cols, chans = cotangent.shape
    obs_dev, feats = observations.shape
    ntiles = lax.axis_size("lon")
    cap = 2 * obs_dev // ntiles
    ncell = lat_rows * lon_cols
    total = ntiles * cap
    counts = tile_counts[0]
    inclusive = jnp.cumsum(counts)
    position = jnp.arange(obs_dev, dtype=jnp.int32)
    gaps = cap - counts
    passed = (position[None, :] >= inclusive[:, None]).astype(jnp.int32)
    slot_of = position + jnp.sum(passed * gaps[:, None], axis=0)
    slots = jnp.arange(total, dtype=jnp.int32)
    place = (slots[:, None] == slot_of[None, :]).astype(BF16)
    high, low = cell_index // 16, cell_index % 16
    extra = jnp.stack([high + 1, low], axis=1).astype(BF16)
    sent = dot(
        place, jnp.concatenate([observations, extra, jnp.zeros((obs_dev, feats - 2), BF16)], axis=1)
    ).astype(BF16)
    codes = sent[:, feats : feats + 2].reshape(ntiles, cap, 2).transpose(0, 2, 1)
    codes = jnp.pad(codes, ((0, 0), (0, 14), (0, feats - cap)))
    block = jnp.concatenate([sent[:, :feats].reshape(ntiles, cap, feats), codes], axis=1)
    got = lax.all_to_all(block, "lon", split_axis=0, concat_axis=0, tiled=True)
    recv_rows = got[:, :cap].reshape(total, feats)
    width = min(256, total)
    recv_cells = (
        (got[:, cap, :cap].astype(jnp.int32) - 1) * 16 + got[:, cap + 1, :cap].astype(jnp.int32)
    ).reshape(total // width, width)

    mean, denom, pre, encoded = pl.pallas_call(
        encode_kernel,
        out_shape=(
            jax.ShapeDtypeStruct((ncell, feats), BF16),
            jax.ShapeDtypeStruct((ncell, feats), F32),
            jax.ShapeDtypeStruct((ncell, chans), F32),
            jax.ShapeDtypeStruct((ncell, chans), BF16),
        ),
        in_specs=[VMEM] * 3,
        out_specs=(VMEM,) * 4,
        scratch_shapes=[pltpu.VMEM((ncell, 2 * feats), F32)],
        compiler_params=pltpu.CompilerParams(vmem_limit_bytes=LIMIT),
        name="encode",
    )(recv_cells, recv_rows, enc_weight)

    gb = shifted(cotangent, ntiles)
    xb = shifted(encoded.reshape(lat_rows, lon_cols, chans), ntiles)
    features, cell_grad, sums = conv_call(
        ntiles, xb, gb, conv_weight.reshape(9 * chans, chans), pre, mean, denom, enc_weight
    )
    slot_grads = pl.pallas_call(
        pick_kernel,
        out_shape=jax.ShapeDtypeStruct((total, feats), BF16),
        in_specs=[VMEM] * 2,
        out_specs=VMEM,
        scratch_shapes=[pltpu.VMEM((feats, ncell), BF16)],
        compiler_params=pltpu.CompilerParams(vmem_limit_bytes=LIMIT),
        name="pick",
    )(recv_cells, cell_grad)
    back_rows = lax.all_to_all(
        slot_grads.reshape(ntiles, cap, feats), "lon", split_axis=0, concat_axis=0, tiled=True
    ).reshape(total, feats)
    take = (slot_of[:, None] == slots[None, :]).astype(BF16)
    obs_grad = dot(take, back_rows).astype(BF16)

    sums = sums[: 9 * chans + feats].astype(F32)
    norm = jnp.sqrt(jnp.sum(sums * sums))
    scale = jnp.minimum(1.0, 1.0 / (norm + 1e-06))
    out = (sums * scale).astype(BF16)
    return (
        features.reshape(cotangent.shape),
        obs_grad,
        out[: 9 * chans].reshape(conv_weight.shape),
        out[9 * chans :],
    )


def solution(mesh):
    return jax.shard_map(
        per_device,
        mesh=mesh,
        in_specs=(
            P(("groups", "lon"), None),
            P(("groups", "lon")),
            P(("groups", "lon"), None),
            P(),
            P(),
            P("groups", "lon", None),
        ),
        out_specs=(
            P("groups", "lon", None),
            P(("groups", "lon"), None),
            P("groups", None, None, None),
            P("groups", None),
        ),
        check_vma=False,
    )
```

```python
import functools

import jax
import jax.numpy as jnp
from jax import lax
from jax.experimental import pallas as pl
from jax.experimental.pallas import tpu as pltpu
from jax.sharding import PartitionSpec as P

F32, BF16 = jnp.float32, jnp.bfloat16
VMEM = pl.BlockSpec(memory_space=pltpu.VMEM)
LIMIT = 48 * 2**20


def dot(a, b):
    return jnp.dot(a, b, preferred_element_type=F32)


def dot_t(a, b):
    return lax.dot_general(a, b, (((1,), (1,)), ((), ())), preferred_element_type=F32)


def encode_kernel(cells_ref, rows_ref, weight_ref, mean_ref, denom_ref, pre_ref, enc_ref, total):
    blocks, width = cells_ref.shape
    ncell, feats = mean_ref.shape
    total[...] = jnp.zeros_like(total)
    ones = jnp.ones((width, feats), BF16)

    def body(i, _):
        ids = lax.broadcasted_iota(jnp.int32, (ncell, width), 0)
        match = (ids == cells_ref[pl.ds(i, 1), :]).astype(F32).astype(BF16)
        rows = rows_ref[pl.ds(pl.multiple_of(i * width, width), width), :]
        total[...] += dot(match, jnp.concatenate([rows, ones], axis=1))
        return 0

    lax.fori_loop(0, blocks, body, 0)
    denom = jnp.maximum(total[:, feats:], 1.0)
    mean = (total[:, :feats] / denom).astype(BF16)
    mean_ref[...] = mean
    denom_ref[...] = denom
    pre = dot(mean, weight_ref[...])
    pre_ref[...] = pre
    enc_ref[...] = (pre * jax.nn.sigmoid(pre)).astype(BF16)


def plan(n, need):
    unit = 16 * n
    units = -(-need // unit)
    streams = min(4, units)
    marks = [units * i // streams for i in range(streams + 1)]
    return [unit * (b - a) for a, b in zip(marks, marks[1:])]


def conv_kernel(
    n, sizes, xb, gb, w, pre_ref, mean_ref, denom_ref, ew_ref, cells_ref,
    feat_ref, back_ref, sum_ref, scale_ref,
    xt, acc, denc, sbuf, rbuf, cell_ref, grad_t, picked, squares,
    rs_send, rs_recv, ag_send, ag_recv, ob_send, ob_recv,
):
    lane = xb.shape[2]
    lat16 = pre_ref.shape[0]
    cols = (xb.shape[1] - lat16) // 2
    feats = mean_ref.shape[1]
    taps = 9
    blocks, width = cells_ref.shape
    cap = picked.shape[0] // n
    me = lax.axis_index("lon")
    levels = n.bit_length() - 1

    def bit_of(k):
        return lax.rem(me // (2**k), 2)

    def partner(k):
        return me + (1 - 2 * bit_of(k)) * (2**k)

    barrier = pltpu.get_barrier_semaphore()

    def greet(i, _):
        pl.semaphore_signal(
            barrier, inc=1, device_id={"lon": lax.rem(me + i, n)},
            device_id_type=pl.DeviceIdType.MESH,
        )
        return 0

    lax.fori_loop(1, n, greet, 0)

    starts, ranges = [], []
    base = 0
    for s, size in enumerate(sizes):
        order = list(range(levels))
        if s % 2 == 0 and levels > 2:
            order = [0] + order[2:] + [1]
        off, length, stages = base, size, []
        for k in order:
            half = length // 2
            b = bit_of(k)
            keep = pl.multiple_of(off + b * half, 16)
            send = pl.multiple_of(off + (1 - b) * half, 16)
            stages.append((k, keep, send, half))
            off, length = keep, half
        starts.append(base)
        ranges.append(stages)
        base += size
    ends = [a + b for a, b in zip(starts, sizes)]

    copies = []
    pos = [0] * len(sizes)
    flying = [None] * len(sizes)

    def send_sum(s, j):
        k, keep, send, half = ranges[s][j]
        sbuf[pl.ds(send, half), :] = acc[pl.ds(send, half), :].astype(BF16)
        copy = pltpu.make_async_remote_copy(
            src_ref=sbuf.at[pl.ds(send, half), :],
            dst_ref=rbuf.at[pl.ds(keep, half), :],
            send_sem=rs_send.at[s, j], recv_sem=rs_recv.at[s, j],
            device_id={"lon": partner(k)}, device_id_type=pl.DeviceIdType.MESH,
        )
        copy.start()
        copies.append(copy)
        flying[s] = copy

    def send_result(s, j):
        k, keep, send, half = ranges[s][j]
        copy = pltpu.make_async_remote_copy(
            src_ref=sum_ref.at[pl.ds(keep, half), :],
            dst_ref=sum_ref.at[pl.ds(keep, half), :],
            send_sem=ag_send.at[s, j], recv_sem=ag_recv.at[s, j],
            device_id={"lon": partner(k)}, device_id_type=pl.DeviceIdType.MESH,
        )
        copy.start()
        copies.append(copy)
        flying[s] = copy

    def add_squares(start, length):
        value = sum_ref[pl.ds(start, length), :].astype(F32)
        squares[...] += jnp.sum(value * value, axis=0, keepdims=True)

    def gradient_copy(i):
        peer = lax.rem(me + i, n)
        return pltpu.make_async_remote_copy(
            src_ref=picked.at[pl.ds(pl.multiple_of(peer * cap, 16), cap), :],
            dst_ref=back_ref.at[pl.ds(pl.multiple_of(me * cap, 16), cap), :],
            send_sem=ob_send.at[i], recv_sem=ob_recv.at[i],
            device_id={"lon": peer}, device_id_type=pl.DeviceIdType.MESH,
        )

    def begin(s):
        send_sum(s, 0)

    def step(s):
        p = pos[s]
        if p >= 2 * levels:
            return
        flying[s].wait_recv()
        if p < levels:
            k, keep, send, half = ranges[s][p]
            value = acc[pl.ds(keep, half), :] + rbuf[pl.ds(send, half), :].astype(F32)
            if p + 1 < levels:
                acc[pl.ds(keep, half), :] = value
                send_sum(s, p + 1)
            else:
                sum_ref[pl.ds(keep, half), :] = value.astype(BF16)
                send_result(s, levels - 1)
                add_squares(keep, half)
        else:
            j = 2 * levels - 1 - p
            if j > 0:
                send_result(s, j - 1)
            k, keep, send, half = ranges[s][j]
            add_squares(send, half)
        pos[s] = p + 1

    squares[...] = jnp.zeros_like(squares)
    for b in range(3):
        xt[b] = xb[b, pl.ds(cols, lat16), :].T
    pl.semaphore_wait(barrier, n - 1)

    def raw_tap(t, _):
        a, b = t // 3, lax.rem(t, 3)
        grad = gb[1, pl.ds(pl.multiple_of((2 - a) * cols, 16), lat16), :]
        acc[pl.ds(pl.multiple_of(t * lane, 16), lane), :] = dot(xt[b], grad)
        return 0

    tile = min(256, lat16)
    tiles = lat16 // tile

    def denc_tile(r, _):
        total = None
        for t in range(taps):
            a, b = t // 3, t % 3
            rows = gb[2 - b, pl.ds(pl.multiple_of((2 - a) * cols + r * tile, 16), tile), :]
            part = dot_t(rows, w[t * lane : (t + 1) * lane, :])
            total = part if total is None else total + part
        here = pl.ds(pl.multiple_of(r * tile, 16), tile)
        pre = pre_ref[here, :]
        sig = jax.nn.sigmoid(pre)
        d_pre = (total * (sig * (1.0 + pre * (1.0 - sig)))).astype(BF16)
        denc[here, :] = d_pre
        cell_ref[here, :] = (dot_t(d_pre, ew_ref[...]) / denom_ref[here, :]).astype(BF16)
        return 0

    def feat_tile(r, _):
        total = None
        for t in range(taps):
            a, b = t // 3, t % 3
            rows = xb[b, pl.ds(pl.multiple_of(a * cols + r * tile, 16), tile), :]
            part = dot(rows, w[t * lane : (t + 1) * lane, :])
            total = part if total is None else total + part
        feat_ref[pl.ds(pl.multiple_of(r * tile, 16), tile), :] = total.astype(BF16)
        return 0

    last = len(sizes) - 1
    done = 0
    for s in range(last):
        upto = min(taps, -(-ends[s] // lane))
        lax.fori_loop(done, upto, raw_tap, 0)
        done = upto
        begin(s)
    if done < taps:
        lax.fori_loop(done, taps, raw_tap, 0)
    for r in range(tiles):
        denc_tile(r, 0)
        for s in range(last):
            step(s)
    acc[taps * lane : taps * lane + feats, :] = lax.dot_general(
        mean_ref[...], denc[...], (((0,), (0,)), ((), ())), preferred_element_type=F32
    )
    if taps * lane + feats < base:
        acc[taps * lane + feats : base, :] = jnp.zeros((base - taps * lane - feats, lane), F32)
    begin(last)

    grad_t[...] = cell_ref[...].T

    def pick(i, _):
        ids = lax.broadcasted_iota(jnp.int32, (lat16, width), 0)
        match = (ids == cells_ref[pl.ds(i, 1), :]).astype(F32).astype(BF16)
        out = dot(grad_t[...], match)
        picked[pl.ds(pl.multiple_of(i * width, width), width), :] = out.T.astype(BF16)
        return 0

    lax.fori_loop(0, blocks, pick, 0)

    def send_gradient(i, _):
        gradient_copy(i).start()
        return 0

    lax.fori_loop(1, n, send_gradient, 0)
    own = pl.ds(pl.multiple_of(me * cap, 16), cap)
    back_ref[own, :] = picked[own, :]
    for r in range(tiles):
        for s in range(last + 1):
            step(s)
        feat_tile(r, 0)
    while min(pos) < 2 * levels:
        for s in range(last + 1):
            step(s)
    norm = jnp.sqrt(jnp.sum(squares[...], axis=1, keepdims=True))
    scale_ref[...] = jnp.broadcast_to(jnp.minimum(1.0, 1.0 / (norm + 1e-06)), scale_ref.shape)

    def finish_gradient(i, _):
        gradient_copy(i).wait()
        return 0

    lax.fori_loop(1, n, finish_gradient, 0)
    for copy in copies:
        copy.wait_send()


def conv_call(n, xb, gb, w, pre, mean, denom, ew, cells):
    lane = xb.shape[2]
    ncell, feats = mean.shape
    need = 9 * lane + feats
    sizes = plan(n, need)
    rows = sum(sizes)
    levels = n.bit_length() - 1
    total = cells.shape[0] * cells.shape[1]
    sems = pltpu.SemaphoreType.DMA((len(sizes), levels))
    return pl.pallas_call(
        functools.partial(conv_kernel, n, sizes),
        out_shape=(
            jax.ShapeDtypeStruct((ncell, lane), BF16),
            jax.ShapeDtypeStruct((total, feats), BF16),
            jax.ShapeDtypeStruct((rows, lane), BF16),
            jax.ShapeDtypeStruct((8, 128), F32),
        ),
        in_specs=[VMEM] * 8,
        out_specs=(VMEM,) * 4,
        scratch_shapes=[
            pltpu.VMEM((3, lane, ncell), BF16),
            pltpu.VMEM((rows, lane), F32),
            pltpu.VMEM((ncell, lane), BF16),
            pltpu.VMEM((rows, lane), BF16),
            pltpu.VMEM((rows, lane), BF16),
            pltpu.VMEM((ncell, feats), BF16),
            pltpu.VMEM((feats, ncell), BF16),
            pltpu.VMEM((total, feats), BF16),
            pltpu.VMEM((1, lane), F32),
            sems, sems, sems, sems,
            pltpu.SemaphoreType.DMA((n,)), pltpu.SemaphoreType.DMA((n,)),
        ],
        compiler_params=pltpu.CompilerParams(
            collective_id=0, has_side_effects=True, vmem_limit_bytes=LIMIT
        ),
        name="conv",
    )(xb, gb, w, pre, mean, denom, ew, cells)


def shifted(grid, ntiles):
    up = [(i, (i + 1) % ntiles) for i in range(ntiles)]
    down = [(j, i) for i, j in up]
    before = lax.ppermute(grid[:, -1:], "lon", up)
    after = lax.ppermute(grid[:, :1], "lon", down)
    views = jnp.stack([
        jnp.concatenate([before, grid[:, :-1]], axis=1),
        grid,
        jnp.concatenate([grid[:, 1:], after], axis=1),
    ])
    views = jnp.pad(views, ((0, 0), (1, 1), (0, 0), (0, 0)))
    return views.reshape(3, -1, grid.shape[-1])


def per_device(observations, cell_index, tile_counts, enc_weight, conv_weight, cotangent):
    lat_rows, lon_cols, chans = cotangent.shape
    obs_dev, feats = observations.shape
    ntiles = lax.axis_size("lon")
    cap = 2 * obs_dev // ntiles
    ncell = lat_rows * lon_cols
    total = ntiles * cap
    counts = tile_counts[0]
    inclusive = jnp.cumsum(counts)
    position = jnp.arange(obs_dev, dtype=jnp.int32)
    gaps = cap - counts
    passed = (position[None, :] >= inclusive[:, None]).astype(jnp.int32)
    slot_of = position + jnp.sum(passed * gaps[:, None], axis=0)
    slots = jnp.arange(total, dtype=jnp.int32)
    place = (slots[:, None] == slot_of[None, :]).astype(BF16)
    high, low = cell_index // 16, cell_index % 16
    extra = jnp.stack([high + 1, low], axis=1).astype(BF16)
    sent = dot(
        place, jnp.concatenate([observations, extra, jnp.zeros((obs_dev, feats - 2), BF16)], axis=1)
    ).astype(BF16)
    codes = sent[:, feats : feats + 2].reshape(ntiles, cap, 2).transpose(0, 2, 1)
    codes = jnp.pad(codes, ((0, 0), (0, 14), (0, feats - cap)))
    block = jnp.concatenate([sent[:, :feats].reshape(ntiles, cap, feats), codes], axis=1)
    got = lax.all_to_all(block, "lon", split_axis=0, concat_axis=0, tiled=True)
    recv_rows = got[:, :cap].reshape(total, feats)
    width = min(256, total)
    recv_cells = (
        (got[:, cap, :cap].astype(jnp.int32) - 1) * 16 + got[:, cap + 1, :cap].astype(jnp.int32)
    ).reshape(total // width, width)

    mean, denom, pre, encoded = pl.pallas_call(
        encode_kernel,
        out_shape=(
            jax.ShapeDtypeStruct((ncell, feats), BF16),
            jax.ShapeDtypeStruct((ncell, feats), F32),
            jax.ShapeDtypeStruct((ncell, chans), F32),
            jax.ShapeDtypeStruct((ncell, chans), BF16),
        ),
        in_specs=[VMEM] * 3,
        out_specs=(VMEM,) * 4,
        scratch_shapes=[pltpu.VMEM((ncell, 2 * feats), F32)],
        compiler_params=pltpu.CompilerParams(vmem_limit_bytes=LIMIT),
        name="encode",
    )(recv_cells, recv_rows, enc_weight)

    gb = shifted(cotangent, ntiles)
    xb = shifted(encoded.reshape(lat_rows, lon_cols, chans), ntiles)
    features, back_rows, sums, scale = conv_call(
        ntiles, xb, gb, conv_weight.reshape(9 * chans, chans), pre, mean, denom, enc_weight,
        recv_cells,
    )
    take = (slot_of[:, None] == slots[None, :]).astype(BF16)
    obs_grad = dot(take, back_rows).astype(BF16)

    factor = scale[0, 0]
    conv_out = (sums[: 9 * chans].astype(F32) * factor).astype(BF16)
    enc_out = (sums[9 * chans : 9 * chans + feats].astype(F32) * factor).astype(BF16)
    return (
        features.reshape(cotangent.shape),
        obs_grad,
        conv_out.reshape(conv_weight.shape),
        enc_out,
    )


def solution(mesh):
    return jax.shard_map(
        per_device,
        mesh=mesh,
        in_specs=(
            P(("groups", "lon"), None),
            P(("groups", "lon")),
            P(("groups", "lon"), None),
            P(),
            P(),
            P("groups", "lon", None),
        ),
        out_specs=(
            P("groups", "lon", None),
            P(("groups", "lon"), None),
            P("groups", None, None, None),
            P("groups", None),
        ),
        check_vma=False,
    )
```

```python
import functools

import jax
import jax.numpy as jnp
from jax import lax
from jax.experimental import pallas as pl
from jax.experimental.pallas import tpu as pltpu
from jax.sharding import PartitionSpec as P

F32, BF16 = jnp.float32, jnp.bfloat16
VMEM = pl.BlockSpec(memory_space=pltpu.VMEM)
LIMIT = 48 * 2**20


def dot(a, b):
    return jnp.dot(a, b, preferred_element_type=F32)


def dot_t(a, b):
    return lax.dot_general(a, b, (((1,), (1,)), ((), ())), preferred_element_type=F32)


def encode_kernel(cells_ref, rows_ref, weight_ref, mean_ref, denom_ref, pre_ref, enc_ref, total):
    blocks, width = cells_ref.shape
    ncell, feats = mean_ref.shape
    total[...] = jnp.zeros_like(total)
    ones = jnp.ones((width, feats), BF16)

    def body(i, _):
        ids = lax.broadcasted_iota(jnp.int32, (ncell, width), 0)
        match = (ids == cells_ref[pl.ds(i, 1), :]).astype(F32).astype(BF16)
        rows = rows_ref[pl.ds(pl.multiple_of(i * width, width), width), :]
        total[...] += dot(match, jnp.concatenate([rows, ones], axis=1))
        return 0

    lax.fori_loop(0, blocks, body, 0)
    denom = jnp.maximum(total[:, feats:], 1.0)
    mean = (total[:, :feats] / denom).astype(BF16)
    mean_ref[...] = mean
    denom_ref[...] = denom
    pre = dot(mean, weight_ref[...])
    pre_ref[...] = pre
    enc_ref[...] = (pre * jax.nn.sigmoid(pre)).astype(BF16)


def plan(n, need):
    unit = 16 * n
    units = -(-need // unit)
    streams = min(7, units)
    marks = [units * i // streams for i in range(streams + 1)]
    return [unit * (b - a) for a, b in zip(marks, marks[1:])]


def conv_kernel(
    n, sizes, xb, gb, w, pre_ref, mean_ref, denom_ref, ew_ref, cells_ref,
    feat_ref, back_ref, sum_ref, scale_ref,
    xt, acc, denc, sbuf, rbuf, cell_ref, grad_t, picked, squares,
    rs_send, rs_recv, ag_send, ag_recv, ob_send, ob_recv,
):
    lane = xb.shape[2]
    lat16 = pre_ref.shape[0]
    cols = (xb.shape[1] - lat16) // 2
    feats = mean_ref.shape[1]
    taps = 9
    blocks, width = cells_ref.shape
    cap = picked.shape[0] // n
    me = lax.axis_index("lon")
    levels = n.bit_length() - 1

    def bit_of(k):
        return lax.rem(me // (2**k), 2)

    def partner(k):
        return me + (1 - 2 * bit_of(k)) * (2**k)

    barrier = pltpu.get_barrier_semaphore()

    def greet(i, _):
        pl.semaphore_signal(
            barrier, inc=1, device_id={"lon": lax.rem(me + i, n)},
            device_id_type=pl.DeviceIdType.MESH,
        )
        return 0

    lax.fori_loop(1, n, greet, 0)

    starts, ranges = [], []
    base = 0
    for s, size in enumerate(sizes):
        order = list(range(levels))
        if s % 3 == 1 and levels > 2:
            order = [0] + order[2:] + [1]
        off, length, stages = base, size, []
        for k in order:
            half = length // 2
            b = bit_of(k)
            keep = pl.multiple_of(off + b * half, 16)
            send = pl.multiple_of(off + (1 - b) * half, 16)
            stages.append((k, keep, send, half))
            off, length = keep, half
        starts.append(base)
        ranges.append(stages)
        base += size
    ends = [a + b for a, b in zip(starts, sizes)]

    copies = []
    pos = [0] * len(sizes)
    flying = [None] * len(sizes)

    def send_sum(s, j):
        k, keep, send, half = ranges[s][j]
        sbuf[pl.ds(send, half), :] = acc[pl.ds(send, half), :].astype(BF16)
        copy = pltpu.make_async_remote_copy(
            src_ref=sbuf.at[pl.ds(send, half), :],
            dst_ref=rbuf.at[pl.ds(keep, half), :],
            send_sem=rs_send.at[s, j], recv_sem=rs_recv.at[s, j],
            device_id={"lon": partner(k)}, device_id_type=pl.DeviceIdType.MESH,
        )
        copy.start()
        copies.append(copy)
        flying[s] = copy

    def send_result(s, j):
        k, keep, send, half = ranges[s][j]
        copy = pltpu.make_async_remote_copy(
            src_ref=sum_ref.at[pl.ds(keep, half), :],
            dst_ref=sum_ref.at[pl.ds(keep, half), :],
            send_sem=ag_send.at[s, j], recv_sem=ag_recv.at[s, j],
            device_id={"lon": partner(k)}, device_id_type=pl.DeviceIdType.MESH,
        )
        copy.start()
        copies.append(copy)
        flying[s] = copy

    def add_squares(start, length):
        value = sum_ref[pl.ds(start, length), :].astype(F32)
        squares[...] += jnp.sum(value * value, axis=0, keepdims=True)

    def gradient_copy(i):
        peer = lax.rem(me + i, n)
        return pltpu.make_async_remote_copy(
            src_ref=picked.at[pl.ds(pl.multiple_of(peer * cap, 16), cap), :],
            dst_ref=back_ref.at[pl.ds(pl.multiple_of(me * cap, 16), cap), :],
            send_sem=ob_send.at[i], recv_sem=ob_recv.at[i],
            device_id={"lon": peer}, device_id_type=pl.DeviceIdType.MESH,
        )

    def begin(s):
        send_sum(s, 0)

    def step(s):
        p = pos[s]
        if p >= 2 * levels:
            return
        flying[s].wait_recv()
        if p < levels:
            k, keep, send, half = ranges[s][p]
            value = acc[pl.ds(keep, half), :] + rbuf[pl.ds(send, half), :].astype(F32)
            if p + 1 < levels:
                acc[pl.ds(keep, half), :] = value
                send_sum(s, p + 1)
            else:
                sum_ref[pl.ds(keep, half), :] = value.astype(BF16)
                send_result(s, levels - 1)
                add_squares(keep, half)
        else:
            j = 2 * levels - 1 - p
            if j > 0:
                send_result(s, j - 1)
            k, keep, send, half = ranges[s][j]
            add_squares(send, half)
        pos[s] = p + 1

    squares[...] = jnp.zeros_like(squares)
    for b in range(3):
        xt[b] = xb[b, pl.ds(cols, lat16), :].T
    pl.semaphore_wait(barrier, n - 1)

    def raw_tap(t, _):
        a, b = t // 3, lax.rem(t, 3)
        grad = gb[1, pl.ds(pl.multiple_of((2 - a) * cols, 16), lat16), :]
        acc[pl.ds(pl.multiple_of(t * lane, 16), lane), :] = dot(xt[b], grad)
        return 0

    tile = min(256, lat16)
    tiles = lat16 // tile

    def denc_tile(r, _):
        total = None
        for t in range(taps):
            a, b = t // 3, t % 3
            rows = gb[2 - b, pl.ds(pl.multiple_of((2 - a) * cols + r * tile, 16), tile), :]
            part = dot_t(rows, w[t * lane : (t + 1) * lane, :])
            total = part if total is None else total + part
        here = pl.ds(pl.multiple_of(r * tile, 16), tile)
        pre = pre_ref[here, :]
        sig = jax.nn.sigmoid(pre)
        d_pre = (total * (sig * (1.0 + pre * (1.0 - sig)))).astype(BF16)
        denc[here, :] = d_pre
        cell_ref[here, :] = (dot_t(d_pre, ew_ref[...]) / denom_ref[here, :]).astype(BF16)
        return 0

    def feat_tile(r, _):
        total = None
        for t in range(taps):
            a, b = t // 3, t % 3
            rows = xb[b, pl.ds(pl.multiple_of(a * cols + r * tile, 16), tile), :]
            part = dot(rows, w[t * lane : (t + 1) * lane, :])
            total = part if total is None else total + part
        feat_ref[pl.ds(pl.multiple_of(r * tile, 16), tile), :] = total.astype(BF16)
        return 0

    last = len(sizes) - 1
    done = 0
    for s in range(last):
        upto = min(taps, -(-ends[s] // lane))
        lax.fori_loop(done, upto, raw_tap, 0)
        done = upto
        begin(s)
    if done < taps:
        lax.fori_loop(done, taps, raw_tap, 0)
    for r in range(tiles):
        denc_tile(r, 0)
        for s in range(last):
            step(s)
    acc[taps * lane : taps * lane + feats, :] = lax.dot_general(
        mean_ref[...], denc[...], (((0,), (0,)), ((), ())), preferred_element_type=F32
    )
    if taps * lane + feats < base:
        acc[taps * lane + feats : base, :] = jnp.zeros((base - taps * lane - feats, lane), F32)
    begin(last)

    grad_t[...] = cell_ref[...].T

    def pick(i, _):
        ids = lax.broadcasted_iota(jnp.int32, (lat16, width), 0)
        match = (ids == cells_ref[pl.ds(i, 1), :]).astype(F32).astype(BF16)
        out = dot(grad_t[...], match)
        picked[pl.ds(pl.multiple_of(i * width, width), width), :] = out.T.astype(BF16)
        return 0

    lax.fori_loop(0, blocks, pick, 0)

    def send_gradient(i, _):
        gradient_copy(i).start()
        return 0

    lax.fori_loop(1, n, send_gradient, 0)
    own = pl.ds(pl.multiple_of(me * cap, 16), cap)
    back_ref[own, :] = picked[own, :]
    for r in range(tiles):
        for s in range(last + 1):
            step(s)
        feat_tile(r, 0)
    while min(pos) < 2 * levels:
        for s in range(last + 1):
            step(s)
    norm = jnp.sqrt(jnp.sum(squares[...], axis=1, keepdims=True))
    scale_ref[...] = jnp.broadcast_to(jnp.minimum(1.0, 1.0 / (norm + 1e-06)), scale_ref.shape)

    def finish_gradient(i, _):
        gradient_copy(i).wait()
        return 0

    lax.fori_loop(1, n, finish_gradient, 0)
    for copy in copies:
        copy.wait_send()


def conv_call(n, xb, gb, w, pre, mean, denom, ew, cells):
    lane = xb.shape[2]
    ncell, feats = mean.shape
    need = 9 * lane + feats
    sizes = plan(n, need)
    rows = sum(sizes)
    levels = n.bit_length() - 1
    total = cells.shape[0] * cells.shape[1]
    sems = pltpu.SemaphoreType.DMA((len(sizes), levels))
    return pl.pallas_call(
        functools.partial(conv_kernel, n, sizes),
        out_shape=(
            jax.ShapeDtypeStruct((ncell, lane), BF16),
            jax.ShapeDtypeStruct((total, feats), BF16),
            jax.ShapeDtypeStruct((rows, lane), BF16),
            jax.ShapeDtypeStruct((8, 128), F32),
        ),
        in_specs=[VMEM] * 8,
        out_specs=(VMEM,) * 4,
        scratch_shapes=[
            pltpu.VMEM((3, lane, ncell), BF16),
            pltpu.VMEM((rows, lane), F32),
            pltpu.VMEM((ncell, lane), BF16),
            pltpu.VMEM((rows, lane), BF16),
            pltpu.VMEM((rows, lane), BF16),
            pltpu.VMEM((ncell, feats), BF16),
            pltpu.VMEM((feats, ncell), BF16),
            pltpu.VMEM((total, feats), BF16),
            pltpu.VMEM((1, lane), F32),
            sems, sems, sems, sems,
            pltpu.SemaphoreType.DMA((n,)), pltpu.SemaphoreType.DMA((n,)),
        ],
        compiler_params=pltpu.CompilerParams(
            collective_id=0, has_side_effects=True, vmem_limit_bytes=LIMIT
        ),
        name="conv",
    )(xb, gb, w, pre, mean, denom, ew, cells)


def shifted(grid, ntiles):
    up = [(i, (i + 1) % ntiles) for i in range(ntiles)]
    down = [(j, i) for i, j in up]
    before = lax.ppermute(grid[:, -1:], "lon", up)
    after = lax.ppermute(grid[:, :1], "lon", down)
    views = jnp.stack([
        jnp.concatenate([before, grid[:, :-1]], axis=1),
        grid,
        jnp.concatenate([grid[:, 1:], after], axis=1),
    ])
    views = jnp.pad(views, ((0, 0), (1, 1), (0, 0), (0, 0)))
    return views.reshape(3, -1, grid.shape[-1])


def per_device(observations, cell_index, tile_counts, enc_weight, conv_weight, cotangent):
    lat_rows, lon_cols, chans = cotangent.shape
    obs_dev, feats = observations.shape
    ntiles = lax.axis_size("lon")
    cap = 2 * obs_dev // ntiles
    ncell = lat_rows * lon_cols
    total = ntiles * cap
    counts = tile_counts[0]
    inclusive = jnp.cumsum(counts)
    position = jnp.arange(obs_dev, dtype=jnp.int32)
    gaps = cap - counts
    passed = (position[None, :] >= inclusive[:, None]).astype(jnp.int32)
    slot_of = position + jnp.sum(passed * gaps[:, None], axis=0)
    slots = jnp.arange(total, dtype=jnp.int32)
    place = (slots[:, None] == slot_of[None, :]).astype(BF16)
    high, low = cell_index // 16, cell_index % 16
    extra = jnp.stack([high + 1, low], axis=1).astype(BF16)
    sent = dot(
        place, jnp.concatenate([observations, extra, jnp.zeros((obs_dev, feats - 2), BF16)], axis=1)
    ).astype(BF16)
    codes = sent[:, feats : feats + 2].reshape(ntiles, cap, 2).transpose(0, 2, 1)
    codes = jnp.pad(codes, ((0, 0), (0, 14), (0, feats - cap)))
    block = jnp.concatenate([sent[:, :feats].reshape(ntiles, cap, feats), codes], axis=1)
    got = lax.all_to_all(block, "lon", split_axis=0, concat_axis=0, tiled=True)
    recv_rows = got[:, :cap].reshape(total, feats)
    width = min(256, total)
    recv_cells = (
        (got[:, cap, :cap].astype(jnp.int32) - 1) * 16 + got[:, cap + 1, :cap].astype(jnp.int32)
    ).reshape(total // width, width)

    mean, denom, pre, encoded = pl.pallas_call(
        encode_kernel,
        out_shape=(
            jax.ShapeDtypeStruct((ncell, feats), BF16),
            jax.ShapeDtypeStruct((ncell, feats), F32),
            jax.ShapeDtypeStruct((ncell, chans), F32),
            jax.ShapeDtypeStruct((ncell, chans), BF16),
        ),
        in_specs=[VMEM] * 3,
        out_specs=(VMEM,) * 4,
        scratch_shapes=[pltpu.VMEM((ncell, 2 * feats), F32)],
        compiler_params=pltpu.CompilerParams(vmem_limit_bytes=LIMIT),
        name="encode",
    )(recv_cells, recv_rows, enc_weight)

    gb = shifted(cotangent, ntiles)
    xb = shifted(encoded.reshape(lat_rows, lon_cols, chans), ntiles)
    features, back_rows, sums, scale = conv_call(
        ntiles, xb, gb, conv_weight.reshape(9 * chans, chans), pre, mean, denom, enc_weight,
        recv_cells,
    )
    take = (slot_of[:, None] == slots[None, :]).astype(BF16)
    obs_grad = dot(take, back_rows).astype(BF16)

    factor = scale[0, 0]
    conv_out = (sums[: 9 * chans].astype(F32) * factor).astype(BF16)
    enc_out = (sums[9 * chans : 9 * chans + feats].astype(F32) * factor).astype(BF16)
    return (
        features.reshape(cotangent.shape),
        obs_grad,
        conv_out.reshape(conv_weight.shape),
        enc_out,
    )


def solution(mesh):
    return jax.shard_map(
        per_device,
        mesh=mesh,
        in_specs=(
            P(("groups", "lon"), None),
            P(("groups", "lon")),
            P(("groups", "lon"), None),
            P(),
            P(),
            P("groups", "lon", None),
        ),
        out_specs=(
            P("groups", "lon", None),
            P(("groups", "lon"), None),
            P("groups", None, None, None),
            P("groups", None),
        ),
        check_vma=False,
    )
```
